32 devices in a mesh: groups: 2 (over x), tensor: 8 (over z, y), replica: 2 (over core).
Axes of the slice: x: 2, y: 2, z: 4, core: 2. Of those that a mesh axis runs over, the one named last changes fastest.
Arguments:
- attention_output_rows: bfloat16 [2, 1536, 8192], P('replica', 'groups', 'tensor'), parts along dimension 1, may hold values from -6 to 6
- residual: bfloat16 [2, 1536, 8192], P('replica', ('groups', 'tensor')), parts along dimension 1, may hold values from -6 to 6
- output_projection_weight: bfloat16 [8192, 8192], P('tensor'), may hold values from -0.0625 to 0.0625
- next_query_weight: bfloat16 [8192, 8192], P(None, 'tensor'), may hold values from -0.0625 to 0.0625
- input_norm_gain: float32 [8192], replicated, may hold values from 0.1 to 1.9
- adapter_down_weight: bfloat16 [64, 8192, 64], P('replica', 'tensor'), may hold values from -0.0625 to 0.0625
- adapter_up_weight: bfloat16 [64, 64, 8192], P('replica', None, 'tensor'), may hold values from -0.75 to 0.75
- request_adapter_index: int32 [2, 8], P('replica', 'groups'), parts along dimension 1, may hold values from 0 to 63
- request_tile_count: int32 [2, 8], P('replica', 'groups'), parts along dimension 1, may hold values from 1 to 6, 12 in all within a row
- request_tail_padding: int32 [2, 8], P('replica', 'groups'), parts along dimension 1, may hold values from 0 to 63
Outputs:
- hidden: bfloat16 [2, 1536, 8192], P('replica', ('groups', 'tensor')), parts along dimension 1
- query: bfloat16 [2, 1536, 8192], P('replica', 'groups', 'tensor'), parts along dimension 1
The draws below stay inside these ranges and needn't reach their ends.
There are 2 independent parts, one for each index of `groups`. The reference program is written for one: setup_inputs(seed, part) draws one part's arguments, and reference() takes and returns one part's arrays. A program takes and returns all parts, laid end to end along the dimension named above; an argument that names none is the same for every part. Nothing has to cross between parts.
All inputs are finite; a program needn't handle non-finite values.
Results may differ from the reference program's by a relative error of at most 0.018.
Values may be sent and summed in bfloat16 or wider, within the bound.
No kernel may reach another device: no remote copies, remote signals or barrier semaphores. Data moves between devices by JAX's collectives and lax.ppermute only.
A program may use at most 128 MiB of HBM per device.

```python
import math
import jax
import jax.numpy as jnp
import numpy as np
from jax import lax

MODEL_WIDTH = 8192
ADAPTER_RANK = 64
TILE = 64
ROWS = 768
ADAPTER_COUNT = 64
TILES = 12
MOST = 6
REQ = 4
REPLICAS = 2
N_TENSOR = 8
N_REPLICA = 2


def with_ends(values, own_key, low, top_value):
    spot = [jax.random.randint(jax.random.fold_in(own_key, axis), (), 0, length) for axis, length in enumerate(values.shape)]
    longest = values.shape.index(max(values.shape))
    neighbour = spot[:longest] + [(spot[longest] + 1) % values.shape[longest]] + spot[longest + 1:]
    return values.at[tuple(spot)].set(low).at[tuple(neighbour)].set(top_value)


def strengthened(drawn, own_key, source, target, parts, factor):
    def block_of(axis_at):
        return (jnp.arange(drawn.shape[axis_at]) // (drawn.shape[axis_at] // parts)).reshape((-1,) + (1,) * (drawn.ndim - 1 - axis_at))

    one_side = jax.random.permutation(own_key, parts)[block_of(target)]
    second = (block_of(target) + parts // 2) % parts
    return jnp.where((block_of(source) == one_side) | (block_of(source) == second), factor * drawn, drawn)


def block_levels(rng, dims, pieces, low, largest):
    loudness, own = 1.0, jax.random.fold_in(rng, 6)
    for axis_at, blocks in pieces:
        heights = jnp.exp(jax.random.uniform(jax.random.fold_in(own, axis_at), (blocks,), jnp.float32, low / len(pieces), largest / len(pieces)))
        loudness = loudness * jnp.repeat(heights, dims[axis_at] // blocks).reshape([-1 if axis == axis_at else 1 for axis in range(len(dims))])
    return loudness


def cumulative_ranks(number_of, slope):
    portions = [(1 << 20) // math.isqrt(grade ** slope) + 1 for grade in range(1, number_of + 1)]
    scale = 1 + sum(portions) // (1 << 30)
    return np.cumsum(np.array([max(1, weight // scale) for weight in portions]))


def ranked_ids(stream_key, extent, count, lean):
    grid = cumulative_ranks(count, lean)
    lot = jax.random.randint(jax.random.fold_in(stream_key, 1), extent, 0, int(grid[count - 1]))
    grade = jnp.searchsorted(jnp.asarray(grid, jnp.int32), lot, side="right")
    return jax.random.permutation(jax.random.fold_in(stream_key, 2), count)[grade].astype(jnp.int32)


def split_up(number_of, total, limit, slope):
    portions = [(1 << 20) // math.isqrt(grade ** slope) + 1 for grade in range(2, number_of + 1)]
    rest, holding = total - limit - (number_of - 1), [1] * (number_of - 1)
    while rest > 0:
        movable = [i for i in range(number_of - 1) if holding[i] < limit]
        pool, remaining = sum([portions[i] for i in movable]), rest
        for i in movable:
            addition = min(limit - holding[i], max(1, remaining * portions[i] // pool), rest)
            holding[i] = holding[i] + addition
            rest = rest - addition
    return np.array([limit] + holding)


def ragged_sizes(own_key, amount, total, bound, lean):
    if amount == 2:
        one = jax.random.randint(own_key, (), max(1, total - bound), min(bound, total - 1) + 1)
        return jnp.stack([one, total - one])
    tallies = jnp.asarray(split_up(amount, total, bound, lean), jnp.int32)
    couples = (amount - 1) // 2
    giver, sink = tallies[1:1 + 2 * couples:2], tallies[2:2 + 2 * couples:2]
    slack = jnp.minimum(giver - 1, bound - sink)
    shifted = jax.random.randint(jax.random.fold_in(own_key, 1), (couples,), 0, 1 << 20) % (slack + 1)
    tallies = tallies.at[1:1 + 2 * couples:2].set(giver - shifted).at[2:2 + 2 * couples:2].set(sink + shifted)
    return tallies[jax.random.permutation(jax.random.fold_in(own_key, 2), amount)]


def bell_draw(own_key, dims, scale, limit, split=(), kind=jnp.bfloat16):
    entries = scale * jax.random.normal(own_key, dims, jnp.float32)
    if split:
        entries = entries * block_levels(own_key, dims, split, -0.22, 0.18)
    return jnp.clip(entries, -limit, limit).astype(kind)


def gaussian_with(rng, shape, deviation, bound, shards, heavy, kind=jnp.bfloat16):
    array = deviation * jax.random.normal(rng, shape, jnp.float32)
    if shards:
        array = array * block_levels(rng, shape, shards, -0.22, 0.18)
    return jnp.clip(strengthened(array, jax.random.fold_in(rng, 3), *heavy), -bound, bound).astype(kind)


def setup_inputs(seed: int = 0, part: int = 0) -> dict:
    arg_keys = jax.random.split(jax.random.key(seed), 11)
    part_keys = jax.random.split(jax.random.fold_in(arg_keys[10], part), 11)
    attention_output_rows = gaussian_with(part_keys[0], (REPLICAS, ROWS, MODEL_WIDTH), 1.0, 6.0, ((0, 2), (2, 8)), (2, 1, 8, 2.0))
    residual = bell_draw(part_keys[1], (REPLICAS, ROWS, MODEL_WIDTH), 1.0, 6.0, ((0, 2), (1, 8)))
    output_projection_weight = bell_draw(arg_keys[2], (MODEL_WIDTH, MODEL_WIDTH), MODEL_WIDTH ** -0.5, 0.0625, ((0, 8),))
    next_query_weight = bell_draw(arg_keys[3], (MODEL_WIDTH, MODEL_WIDTH), MODEL_WIDTH ** -0.5, 0.0625, ((1, 8),))
    input_norm_gain = jnp.clip(1.0 + 0.18 * jax.random.normal(arg_keys[4], (MODEL_WIDTH,), jnp.float32), 0.1, 1.9)
    adapter_down_weight = bell_draw(arg_keys[5], (ADAPTER_COUNT, MODEL_WIDTH, ADAPTER_RANK), MODEL_WIDTH ** -0.5, 0.0625, ((0, 2), (1, 8)))
    adapter_up_weight = bell_draw(arg_keys[6], (ADAPTER_COUNT, ADAPTER_RANK, MODEL_WIDTH), ADAPTER_RANK ** -0.5, 0.75, ((0, 2), (2, 8)))
    request_adapter_index = with_ends(ranked_ids(part_keys[7], (REPLICAS, REQ), ADAPTER_COUNT, 2), jax.random.fold_in(part_keys[7], 3), 0, ADAPTER_COUNT - 1).astype(jnp.int32)
    request_tile_count = jax.vmap(lambda own: ragged_sizes(own, REQ, TILES, MOST, 2))(jax.random.split(part_keys[8], REPLICAS)).reshape((REPLICAS, REQ)).astype(jnp.int32)
    request_tail_padding = with_ends(jax.random.randint(part_keys[9], (REPLICAS, REQ), 0, TILE), jax.random.fold_in(part_keys[9], 1), 0, TILE - 1).astype(jnp.int32)
    return {"attention_output_rows": attention_output_rows, "residual": residual, "output_projection_weight": output_projection_weight, "next_query_weight": next_query_weight, "input_norm_gain": input_norm_gain, "adapter_down_weight": adapter_down_weight, "adapter_up_weight": adapter_up_weight, "request_adapter_index": request_adapter_index, "request_tile_count": request_tile_count, "request_tail_padding": request_tail_padding}


adapter_scale = 2.0

def row_maps(tiles, pad):
    sizes = (tiles * TILE).astype(jnp.int32)
    ends = jnp.cumsum(sizes).astype(jnp.int32)
    starts = ends - sizes
    place = jnp.arange(ROWS, dtype=jnp.int32)[:, None]
    inside = (place >= starts[None, :]) & (place < ends[None, :])
    used = place < (ends - pad.astype(jnp.int32))[None, :]
    member = jnp.where(inside, 1.0, 0.0).astype(jnp.float32)
    valid_row_mask = lax.optimization_barrier(jnp.sum(jnp.where(inside & used, 1.0, 0.0), axis=1)).astype(jnp.float32)
    return (member, valid_row_mask)

def normalize(hidden, input_norm_gain):
    values = hidden.astype(jnp.float32)
    scale = lax.rsqrt(lax.optimization_barrier(jnp.mean(values * values, axis=-1, keepdims=True)) + 1e-05)
    return (values * scale * input_norm_gain.astype(jnp.float32)[None, :]).astype(jnp.bfloat16)

def reference(attention_output_rows, residual, output_projection_weight, next_query_weight, input_norm_gain, adapter_down_weight, adapter_up_weight, request_adapter_index, request_tile_count, request_tail_padding):
    width = MODEL_WIDTH // N_TENSOR
    hidden_list = []
    query_list = []
    for block in range(N_REPLICA):
        total = jnp.zeros((ROWS, MODEL_WIDTH), jnp.float32)
        for piece in range(N_TENSOR):
            lower = piece * width
            term = jnp.dot(attention_output_rows[block, :, lower:lower + width], output_projection_weight[lower:lower + width, :], preferred_element_type=jnp.float32).astype(jnp.bfloat16)
            total = total + lax.optimization_barrier(term).astype(jnp.float32)
        hidden = (residual[block].astype(jnp.float32) + total).astype(jnp.bfloat16)
        normed = normalize(hidden, input_norm_gain)
        member, valid_row_mask = row_maps(request_tile_count[block], request_tail_padding[block])
        picked_adapter = request_adapter_index[block].astype(jnp.int32)
        tile_count = picked_adapter.shape[0]
        down_factor = jnp.transpose(adapter_down_weight[picked_adapter], (1, 0, 2)).reshape(MODEL_WIDTH, tile_count * ADAPTER_RANK)
        up_factor = adapter_up_weight[picked_adapter].reshape(tile_count * ADAPTER_RANK, MODEL_WIDTH)
        product = jnp.dot(normed, down_factor, preferred_element_type=jnp.float32)
        low = lax.optimization_barrier(jnp.sum(product.reshape(ROWS, tile_count, ADAPTER_RANK) * member[:, :, None], axis=1)).astype(jnp.bfloat16)
        spread = (low.astype(jnp.float32)[:, None, :] * member[:, :, None]).reshape(ROWS, tile_count * ADAPTER_RANK).astype(jnp.bfloat16)
        adapter_update = jnp.dot(spread, up_factor, preferred_element_type=jnp.float32)
        query_without_adapter = jnp.dot(normed, next_query_weight, preferred_element_type=jnp.float32)
        query = ((query_without_adapter + adapter_scale * adapter_update) * valid_row_mask[:, None]).astype(jnp.bfloat16)
        hidden_list.append(hidden)
        query_list.append(query)
    return (jnp.stack(hidden_list, 0), jnp.stack(query_list, 0))
```

```python
import jax
import jax.numpy as jnp
from jax import lax
from jax.sharding import PartitionSpec as P

TILE = 64
STREAMS = 2
adapter_scale = 2.0


def tied(values, after):
    return lax.optimization_barrier((values, after))[0]


def ring_order(count):
    if count % 2 or count > 8:
        return list(range(count))
    return list(range(0, count, 2)) + list(range(count - 1, 0, -2))


def swapped(values, replicas, shift):
    return lax.ppermute(values, "replica", [(i, (i + shift) % replicas) for i in range(replicas)])


def fetched(store, picked, asked):
    resident = store.shape[0]
    replicas = lax.axis_size("replica")
    mine = lax.axis_index("replica")
    holder = picked // resident

    def held(wanted):
        here = wanted // resident == mine
        return store[jnp.where(here, wanted - mine * resident, 0)]

    factor = held(picked)
    for shift in range(1, replicas):
        from_peer = (holder == (mine - shift) % replicas)[:, None, None]
        factor = jnp.where(from_peer, swapped(held(asked[shift]), replicas, shift), factor)
    return factor


def on_device(
    attention_output_rows,
    residual,
    output_projection_weight,
    next_query_weight,
    input_norm_gain,
    adapter_down_weight,
    adapter_up_weight,
    request_adapter_index,
    request_tile_count,
    request_tail_padding,
):
    features = attention_output_rows[0]
    total_rows = features.shape[0]
    depth, model = output_projection_weight.shape
    width = next_query_weight.shape[1]
    rank = adapter_down_weight.shape[2]
    count = lax.axis_size("tensor")
    index = lax.axis_index("tensor")
    rows = total_rows // count
    order = ring_order(count)

    def wrapped(at):
        return at & (count - 1) if count & (count - 1) == 0 else lax.rem(at, count)

    if order[-1] == 1:
        place = jnp.where(index & 1 == 1, count - 1 - index // 2, index // 2)
    else:
        place = index

    def first_row(at):
        at = wrapped(at + 2 * count)
        if order[-1] == 1:
            at = jnp.where(at < count // 2, 2 * at, 2 * (count - 1 - at) + 1)
        return at * rows

    def hop(values, way):
        pairs = [(order[i], order[(i + way) % count]) for i in range(count)]
        return lax.ppermute(values, "tensor", pairs)

    ways = (1, -1)
    half = model // 2
    piece = half // STREAMS

    def terms(way, at, after=None):
        source = features if after is None else tied(features, after)
        block = lax.dynamic_slice_in_dim(source, first_row(at), rows, 0)
        lower = 0 if way == 1 else half
        product = jnp.dot(
            block, output_projection_weight[:, lower : lower + half], preferred_element_type=jnp.float32
        ).astype(jnp.bfloat16)
        product = lax.optimization_barrier(product)
        return [product[:, i * piece : (i + 1) * piece] for i in range(STREAMS)]

    picked_adapter = request_adapter_index[0]
    requests = picked_adapter.shape[0]

    replicas = lax.axis_size("replica")
    asked = {shift: swapped(picked_adapter, replicas, -shift) for shift in range(1, replicas)}
    down_factor = up_factor = None

    held = {way: terms(way, place - way) for way in ways}
    summed = []
    for step in range(count - 1):
        if step == 2:
            down_factor = fetched(tied(adapter_down_weight, held[1][0]), picked_adapter, asked)
        if step == 3:
            held[1][0], down_factor = lax.optimization_barrier((held[1][0], down_factor))
            up_factor = fetched(tied(adapter_up_weight, held[1][0]), picked_adapter, asked)
        if step == 4:
            held[1][0], up_factor = lax.optimization_barrier((held[1][0], up_factor))
        own = {way: terms(way, place - way * (2 + step), held[way][0]) for way in ways}
        for way in ways:
            for i in range(STREAMS):
                total = hop(held[way][i], way).astype(jnp.float32) + own[way][i].astype(jnp.float32)
                if step < count - 2:
                    held[way][i] = total.astype(jnp.bfloat16)
                else:
                    summed.append(total)
    hidden = (residual[0].astype(jnp.float32) + jnp.concatenate(summed, axis=1)).astype(jnp.bfloat16)
    values = hidden.astype(jnp.float32)
    scale = lax.rsqrt(jnp.mean(values * values, axis=-1, keepdims=True) + 1e-05)
    normed = (values * scale * input_norm_gain[None, :]).astype(jnp.bfloat16)

    sizes = request_tile_count[0] * TILE
    ends = jnp.cumsum(sizes)
    starts_of = ends - sizes

    def members(first, number):
        at = first + lax.broadcasted_iota(jnp.int32, (number, 1), 0)
        inside = (at >= jnp.repeat(starts_of, rank)[None, :]) & (at < jnp.repeat(ends, rank)[None, :])
        return jnp.where(inside, 1.0, 0.0).astype(jnp.float32)

    flat_down = jnp.transpose(down_factor, (1, 0, 2)).reshape(depth, requests * rank)
    base = jnp.zeros((total_rows, width), jnp.float32)
    low = jnp.zeros((total_rows, rank), jnp.float32)

    def put(whole, values, starts):
        share = values.shape[0] // len(starts)
        for i, start in enumerate(starts):
            whole = lax.dynamic_update_slice_in_dim(whole, values[i * share : (i + 1) * share], start, 0)
        return whole

    def first_products(blocks, starts):
        share = blocks[0].shape[0] // len(starts)
        lower = jnp.where(index * depth < half, index * depth, index * depth - half)
        parts = [lax.dynamic_slice_in_dim(block, lower, depth, 1) for block in blocks]
        part = jnp.where(index * depth < half, parts[0], parts[1])
        product = jnp.dot(part, flat_down, preferred_element_type=jnp.float32)
        product = product * jnp.concatenate([members(start, share) for start in starts], axis=0)
        return sum(product[:, j * rank : (j + 1) * rank] for j in range(requests))

    def query_product(block, i):
        return jnp.dot(
            block, next_query_weight[i * half : (i + 1) * half], preferred_element_type=jnp.float32
        )

    upper = rows // 2
    blocks = [normed[:, i * half : (i + 1) * half] for i in range(2)]
    held = {1: [c[:upper] for c in blocks], -1: [c[upper:] for c in blocks]}
    starts = [first_row(place)]
    for step in range(count):
        if step < count - 1:
            arrived = {way: [hop(held[way][i], way) for i in range(2)] for way in ways}
        low = put(low, first_products(blocks, starts), starts)
        products = [query_product(blocks[i], i) for i in range(2)]
        base = put(base, products[0] + products[1], starts)
        if step < count - 1:
            for i in range(2):
                (held[1][i], held[-1][i]), products[i] = lax.optimization_barrier(
                    ((arrived[1][i], arrived[-1][i]), products[i])
                )
            blocks = [jnp.concatenate([held[way][i] for way in ways], axis=0) for i in range(2)]
            starts = [first_row(place - 1 - step), first_row(place + 1 + step) + upper]

    distance = 1
    low = low.astype(jnp.bfloat16)
    if count & (count - 1) == 0:
        while distance < count:
            other = lax.ppermute(low, "tensor", [(i, i ^ distance) for i in range(count)])
            low = (low.astype(jnp.float32) + other.astype(jnp.float32)).astype(jnp.bfloat16)
            distance *= 2
    else:
        low = lax.psum(low, "tensor")
    member = members(0, total_rows)
    spread = (jnp.concatenate([low] * requests, axis=1).astype(jnp.float32) * member).astype(jnp.bfloat16)
    adapter_update = jnp.dot(
        spread, up_factor.reshape(requests * rank, width), preferred_element_type=jnp.float32
    )
    at = lax.broadcasted_iota(jnp.int32, (total_rows, requests), 0)
    used = (at >= starts_of[None, :]) & (at < (ends - request_tail_padding[0])[None, :])
    live = jnp.sum(jnp.where(used, 1.0, 0.0).astype(jnp.float32), axis=1)
    query = ((base + adapter_scale * adapter_update) * live[:, None]).astype(jnp.bfloat16)
    return (hidden[None], query[None])


def solution(mesh):
    in_specs = (
        P("replica", "groups", "tensor"),
        P("replica", ("groups", "tensor"), None),
        P("tensor", None),
        P(None, "tensor"),
        P(),
        P("replica", "tensor", None),
        P("replica", None, "tensor"),
        P("replica", "groups"),
        P("replica", "groups"),
        P("replica", "groups"),
    )
    out_specs = (P("replica", ("groups", "tensor"), None), P("replica", "groups", "tensor"))
    return jax.shard_map(
        on_device, mesh=mesh, in_specs=in_specs, out_specs=out_specs, check_vma=False
    )
```

```python
import jax
import jax.numpy as jnp
from jax import lax
from jax.experimental import pallas as pl
from jax.experimental.pallas import tpu as pltpu
from jax.sharding import PartitionSpec as P

TILE = 64
STREAMS = 2
OWN_STEP = 4
adapter_scale = 2.0


def tied(values, after):
    return lax.optimization_barrier((values, after))[0]


def ring_order(count):
    if count % 2 or count > 8:
        return list(range(count))
    return list(range(0, count, 2)) + list(range(count - 1, 0, -2))


def swapped(values, replicas, shift):
    return lax.ppermute(values, "replica", [(i, (i + shift) % replicas) for i in range(replicas)])


def row_maps_kernel(requests, rank, tiles_ref, padding_ref, member_ref, live_ref):
    at = lax.broadcasted_iota(jnp.int32, member_ref.shape, 0)
    column = lax.broadcasted_iota(jnp.int32, member_ref.shape, 1)
    member = jnp.zeros(member_ref.shape, jnp.float32)
    row = lax.broadcasted_iota(jnp.int32, live_ref.shape, 0)
    live = jnp.zeros(live_ref.shape, jnp.float32)
    start = jnp.int32(0)
    for j in range(requests):
        end = start + tiles_ref[j] * TILE
        mine = (column >= j * rank) & (column < (j + 1) * rank)
        member = jnp.where(mine & (at >= start) & (at < end), 1.0, member)
        live = jnp.where((row >= start) & (row < end - padding_ref[j]), 1.0, live)
        start = end
    member_ref[...] = member
    live_ref[...] = live


def row_maps(tile_count, padding, total_rows, rank):
    requests = tile_count.shape[0]
    return pl.pallas_call(
        lambda *refs: row_maps_kernel(requests, rank, *refs),
        in_specs=[pl.BlockSpec(memory_space=pltpu.SMEM)] * 2,
        out_specs=[pl.BlockSpec(memory_space=pltpu.VMEM)] * 2,
        out_shape=[
            jax.ShapeDtypeStruct((total_rows, requests * rank), jnp.float32),
            jax.ShapeDtypeStruct((total_rows, 128), jnp.float32),
        ],
    )(tile_count, padding)


def fetched(store, picked, asked):
    resident = store.shape[0]
    replicas = lax.axis_size("replica")
    mine = lax.axis_index("replica")
    holder = picked // resident

    def held(wanted):
        here = wanted // resident == mine
        return store[jnp.where(here, wanted - mine * resident, 0)]

    factor = held(picked)
    for shift in range(1, replicas):
        from_peer = (holder == (mine - shift) % replicas)[:, None, None]
        factor = jnp.where(from_peer, swapped(held(asked[shift]), replicas, shift), factor)
    return factor


def on_device(
    attention_output_rows,
    residual,
    output_projection_weight,
    next_query_weight,
    input_norm_gain,
    adapter_down_weight,
    adapter_up_weight,
    request_adapter_index,
    request_tile_count,
    request_tail_padding,
):
    features = attention_output_rows[0]
    total_rows = features.shape[0]
    depth, model = output_projection_weight.shape
    width = next_query_weight.shape[1]
    rank = adapter_down_weight.shape[2]
    count = lax.axis_size("tensor")
    index = lax.axis_index("tensor")
    rows = total_rows // count
    order = ring_order(count)

    def wrapped(at):
        return at & (count - 1) if count & (count - 1) == 0 else lax.rem(at, count)

    if order[-1] == 1:
        place = jnp.where(index & 1 == 1, count - 1 - index // 2, index // 2)
    else:
        place = index

    def block_at(at):
        at = wrapped(at + 2 * count)
        if order[-1] == 1:
            at = jnp.where(at < count // 2, 2 * at, 2 * (count - 1 - at) + 1)
        return at

    def first_row(at):
        return block_at(at) * rows

    def hop(values, way):
        pairs = [(order[i], order[(i + way) % count]) for i in range(count)]
        return lax.ppermute(values, "tensor", pairs)

    ways = (1, -1)
    half = model // 2
    piece = half // STREAMS

    def block_of(product, way, step):
        return lax.dynamic_slice_in_dim(product, first_row(place - way * (1 + step)), rows, 0)

    picked_adapter = request_adapter_index[0]
    requests = picked_adapter.shape[0]

    replicas = lax.axis_size("replica")
    asked = {shift: swapped(picked_adapter, replicas, -shift) for shift in range(1, replicas)}
    down_factor = up_factor = None

    own, held, before = {}, {}, None
    for i in range(STREAMS):
        for way in ways:
            source = features if before is None else tied(features, before)
            lower = (0 if way == 1 else half) + i * piece
            weight = output_projection_weight[:, lower : lower + piece]
            before = jnp.dot(source, weight, preferred_element_type=jnp.float32).astype(jnp.bfloat16)
            own[way, i], held[way, i] = before, block_of(before, way, 0)
    for step in range(count - 1):
        if step == 2:
            down_factor = fetched(tied(adapter_down_weight, held[1, 0]), picked_adapter, asked)
        if step == 3:
            held[1, 0], down_factor = lax.optimization_barrier((held[1, 0], down_factor))
            up_factor = fetched(tied(adapter_up_weight, held[1, 0]), picked_adapter, asked)
        if step == 4:
            held[1, 0], up_factor = lax.optimization_barrier((held[1, 0], up_factor))
            maps = tied((request_tile_count[0], request_tail_padding[0]), held[1, 0])
            member, live = row_maps(*maps, total_rows, rank)
        if step == 5:
            held[1, 0], member, live = lax.optimization_barrier((held[1, 0], member, live))
        for i in range(STREAMS):
            for way in ways:
                term = block_of(own[way, i], way, step + 1).astype(jnp.float32)
                arrived = hop(held[way, i], way).astype(jnp.float32) + term
                held[way, i] = arrived if step == count - 2 else arrived.astype(jnp.bfloat16)
    hidden = (residual[0].astype(jnp.float32) + jnp.concatenate([held[way, i] for way in ways for i in range(STREAMS)], axis=1)).astype(jnp.bfloat16)
    values = hidden.astype(jnp.float32)
    scale = lax.rsqrt(jnp.mean(values * values, axis=-1, keepdims=True) + 1e-05)
    normed = (values * scale * input_norm_gain[None, :]).astype(jnp.bfloat16)

    upper = rows // 2
    held = {}
    for i in range(2):
        held[1, i] = normed[:upper, i * half : (i + 1) * half]
        held[-1, i] = normed[upper:, i * half : (i + 1) * half]
    arrived = {key: hop(values, key[0]) for key, values in held.items()}
    flat_down = jnp.transpose(down_factor, (1, 0, 2)).reshape(depth, requests * rank)
    base = jnp.zeros((total_rows, width), jnp.float32)

    def put(whole, values, starts):
        share = values.shape[0] // len(starts)
        for i, start in enumerate(starts):
            whole = lax.dynamic_update_slice_in_dim(whole, values[i * share : (i + 1) * share], start, 0)
        return whole

    def columns(blocks, owner):
        lower = jnp.where(owner * depth < half, owner * depth, owner * depth - half)
        parts = [lax.dynamic_slice_in_dim(block, lower, depth, 1) for block in blocks]
        return jnp.where(owner * depth < half, parts[0], parts[1])

    def first_products(blocks, starts):
        share = blocks[0].shape[0] // len(starts)
        product = jnp.dot(columns(blocks, index), flat_down, preferred_element_type=jnp.float32)
        product = product * jnp.concatenate(
            [lax.dynamic_slice_in_dim(member, start, share, 0) for start in starts], axis=0
        )
        return sum(product[:, j * rank : (j + 1) * rank] for j in range(requests))

    def starts_at(step):
        return [first_row(place - step), first_row(place + step) + upper]

    def query_product(block, i):
        return jnp.dot(
            block, next_query_weight[i * half : (i + 1) * half], preferred_element_type=jnp.float32
        )

    def pair(values, i):
        return jnp.concatenate([values[1, i], values[-1, i]], axis=0)

    mine = [pair(held, i) for i in range(2)]
    low = jnp.zeros((total_rows, rank), jnp.float32)
    for step in range(1, count):
        held, starts = arrived, starts_at(step)
        if step < count - 1:
            arrived = {key: hop(values, key[0]) for key, values in held.items()}
        blocks = [pair(held, i) for i in range(2)]
        low = put(low, first_products(blocks, starts), starts)
        products = [query_product(blocks[i], i) for i in range(2)]
        if step < count - 1:
            base = put(base, products[0] + products[1], starts)
        if step == min(OWN_STEP, count - 2):
            mine = [tied(mine[i], products[i]) for i in range(2)]
            low = put(low, first_products(mine, starts_at(0)), starts_at(0))
            base = put(base, query_product(mine[0], 0) + query_product(mine[1], 1), starts_at(0))
        if step < count - 1:
            for i in range(2):
                (arrived[1, i], arrived[-1, i]), products[i] = lax.optimization_barrier(
                    ((arrived[1, i], arrived[-1, i]), products[i])
                )

    low = jnp.concatenate([low[: total_rows // 2], low[total_rows // 2 :]], axis=1).astype(jnp.bfloat16)
    if count & (count - 1) == 0:
        distance = 1
        while distance < count:
            other = lax.ppermute(low, "tensor", [(i, i ^ distance) for i in range(count)])
            low = (low.astype(jnp.float32) + other.astype(jnp.float32)).astype(jnp.bfloat16)
            distance *= 2
    else:
        low = lax.psum(low, "tensor")
    low = jnp.concatenate([low[:, :rank], low[:, rank:]], axis=0)
    base = put(base, products[0] + products[1], starts)
    spread = (jnp.concatenate([low] * requests, axis=1).astype(jnp.float32) * member).astype(jnp.bfloat16)
    adapter_update = jnp.dot(
        spread, up_factor.reshape(requests * rank, width), preferred_element_type=jnp.float32
    )
    query = ((base + adapter_scale * adapter_update) * live[:, :1]).astype(jnp.bfloat16)
    return (hidden[None], query[None])


def solution(mesh):
    in_specs = (
        P("replica", "groups", "tensor"),
        P("replica", ("groups", "tensor"), None),
        P("tensor", None),
        P(None, "tensor"),
        P(),
        P("replica", "tensor", None),
        P("replica", None, "tensor"),
        P("replica", "groups"),
        P("replica", "groups"),
        P("replica", "groups"),
    )
    out_specs = (P("replica", ("groups", "tensor"), None), P("replica", "groups", "tensor"))
    return jax.shard_map(
        on_device, mesh=mesh, in_specs=in_specs, out_specs=out_specs, check_vma=False
    )
```

```python
import jax
import jax.numpy as jnp
from jax import lax
from jax.experimental import pallas as pl
from jax.experimental.pallas import tpu as pltpu
from jax.sharding import PartitionSpec as P

TILE = 64
STREAMS = 2
OWN_STEP = 4
adapter_scale = 2.0


def tied(values, after):
    return lax.optimization_barrier((values, after))[0]


def ring_order(count):
    if count % 2 or count > 8:
        return list(range(count))
    return list(range(0, count, 2)) + list(range(count - 1, 0, -2))


def swapped(values, replicas, shift):
    return lax.ppermute(values, "replica", [(i, (i + shift) % replicas) for i in range(replicas)])


def row_maps_kernel(requests, rank, tiles_ref, padding_ref, member_ref, live_ref):
    at = lax.broadcasted_iota(jnp.int32, member_ref.shape, 0)
    column = lax.broadcasted_iota(jnp.int32, member_ref.shape, 1)
    member = jnp.zeros(member_ref.shape, jnp.float32)
    row = lax.broadcasted_iota(jnp.int32, live_ref.shape, 0)
    live = jnp.zeros(live_ref.shape, jnp.float32)
    start = jnp.int32(0)
    for j in range(requests):
        end = start + tiles_ref[j] * TILE
        mine = (column >= j * rank) & (column < (j + 1) * rank)
        member = jnp.where(mine & (at >= start) & (at < end), 1.0, member)
        live = jnp.where((row >= start) & (row < end - padding_ref[j]), 1.0, live)
        start = end
    member_ref[...] = member
    live_ref[...] = live


def row_maps(tile_count, padding, total_rows, rank):
    requests = tile_count.shape[0]
    return pl.pallas_call(
        lambda *refs: row_maps_kernel(requests, rank, *refs),
        in_specs=[pl.BlockSpec(memory_space=pltpu.SMEM)] * 2,
        out_specs=[pl.BlockSpec(memory_space=pltpu.VMEM)] * 2,
        out_shape=[
            jax.ShapeDtypeStruct((total_rows, requests * rank), jnp.float32),
            jax.ShapeDtypeStruct((total_rows, 128), jnp.float32),
        ],
    )(tile_count, padding)


def fetched(store, picked, asked):
    resident = store.shape[0]
    replicas = lax.axis_size("replica")
    mine = lax.axis_index("replica")
    holder = picked // resident

    def held(wanted):
        here = wanted // resident == mine
        return store[jnp.where(here, wanted - mine * resident, 0)]

    factor = held(picked)
    for shift in range(1, replicas):
        from_peer = (holder == (mine - shift) % replicas)[:, None, None]
        factor = jnp.where(from_peer, swapped(held(asked[shift]), replicas, shift), factor)
    return factor


def on_device(
    attention_output_rows,
    residual,
    output_projection_weight,
    next_query_weight,
    input_norm_gain,
    adapter_down_weight,
    adapter_up_weight,
    request_adapter_index,
    request_tile_count,
    request_tail_padding,
):
    features = attention_output_rows[0]
    total_rows = features.shape[0]
    depth, model = output_projection_weight.shape
    width = next_query_weight.shape[1]
    rank = adapter_down_weight.shape[2]
    count = lax.axis_size("tensor")
    index = lax.axis_index("tensor")
    rows = total_rows // count
    order = ring_order(count)

    def wrapped(at):
        return at & (count - 1) if count & (count - 1) == 0 else lax.rem(at, count)

    if order[-1] == 1:
        place = jnp.where(index & 1 == 1, count - 1 - index // 2, index // 2)
    else:
        place = index

    def block_at(at):
        at = wrapped(at + 2 * count)
        if order[-1] == 1:
            at = jnp.where(at < count // 2, 2 * at, 2 * (count - 1 - at) + 1)
        return at

    def first_row(at):
        return block_at(at) * rows

    def hop(values, way):
        pairs = [(order[i], order[(i + way) % count]) for i in range(count)]
        return lax.ppermute(values, "tensor", pairs)

    ways = (1, -1)
    half = model // 2
    piece = half // STREAMS

    def block_of(product, way, step):
        return lax.dynamic_slice_in_dim(product, first_row(place - way * (1 + step)), rows, 0)

    picked_adapter = request_adapter_index[0]
    requests = picked_adapter.shape[0]

    replicas = lax.axis_size("replica")
    asked = {shift: swapped(picked_adapter, replicas, -shift) for shift in range(1, replicas)}
    down_factor = up_factor = None

    own, held, before = {}, {}, None
    for i in range(STREAMS):
        for way in ways:
            source = features if before is None else tied(features, before)
            lower = (0 if way == 1 else half) + i * piece
            weight = output_projection_weight[:, lower : lower + piece]
            before = jnp.dot(source, weight, preferred_element_type=jnp.float32).astype(jnp.bfloat16)
            own[way, i], held[way, i] = before, block_of(before, way, 0)
    for step in range(count - 1):
        if step == 2:
            down_factor = fetched(tied(adapter_down_weight, held[-1,0]), picked_adapter, asked)
        if step == 3:
            up_factor = fetched(tied(adapter_up_weight, held[-1,0]), picked_adapter, asked)
        if step == 4:
            maps = tied((request_tile_count[0], request_tail_padding[0]), held[-1,0])
            member, live = row_maps(*maps, total_rows, rank)
        if step == 4:
            held[-1,0], down_factor = lax.optimization_barrier((held[-1,0], down_factor))
        if step == 5:
            held[-1,0], up_factor = lax.optimization_barrier((held[-1,0], up_factor))
        if step == 6:
            held[-1,0], member, live = lax.optimization_barrier((held[-1,0], member, live))
        for i in range(STREAMS):
            for way in ways:
                term = block_of(own[way, i], way, step + 1).astype(jnp.float32)
                arrived = hop(held[way, i], way).astype(jnp.float32) + term
                held[way, i] = arrived if step == count - 2 else arrived.astype(jnp.bfloat16)
    hidden = (residual[0].astype(jnp.float32) + jnp.concatenate([held[way, i] for way in ways for i in range(STREAMS)], axis=1)).astype(jnp.bfloat16)
    values = hidden.astype(jnp.float32)
    scale = lax.rsqrt(jnp.mean(values * values, axis=-1, keepdims=True) + 1e-05)
    normed = (values * scale * input_norm_gain[None, :]).astype(jnp.bfloat16)

    upper = rows // 2
    held = {}
    for i in range(2):
        held[1, i] = normed[:upper, i * half : (i + 1) * half]
        held[-1, i] = normed[upper:, i * half : (i + 1) * half]
    arrived = {key: hop(values, key[0]) for key, values in held.items()}
    (arrived[1, 0], arrived[-1, 0]), hidden = lax.optimization_barrier(((arrived[1, 0], arrived[-1, 0]), hidden))
    flat_down = jnp.transpose(down_factor, (1, 0, 2)).reshape(depth, requests * rank)
    base = jnp.zeros((total_rows, width), jnp.float32)

    def put(whole, values, starts):
        share = values.shape[0] // len(starts)
        for i, start in enumerate(starts):
            whole = lax.dynamic_update_slice_in_dim(whole, values[i * share : (i + 1) * share], start, 0)
        return whole

    def columns(blocks, owner):
        lower = jnp.where(owner * depth < half, owner * depth, owner * depth - half)
        parts = [lax.dynamic_slice_in_dim(block, lower, depth, 1) for block in blocks]
        return jnp.where(owner * depth < half, parts[0], parts[1])

    def first_products(blocks, starts):
        share = blocks[0].shape[0] // len(starts)
        product = jnp.dot(columns(blocks, index), flat_down, preferred_element_type=jnp.float32)
        product = product * jnp.concatenate(
            [lax.dynamic_slice_in_dim(member, start, share, 0) for start in starts], axis=0
        )
        return sum(product[:, j * rank : (j + 1) * rank] for j in range(requests))

    def starts_at(step):
        return [first_row(place - step), first_row(place + step) + upper]

    def query_product(block, i):
        return jnp.dot(
            block, next_query_weight[i * half : (i + 1) * half], preferred_element_type=jnp.float32
        )

    def pair(values, i):
        return jnp.concatenate([values[1, i], values[-1, i]], axis=0)

    mine = [pair(held, i) for i in range(2)]
    low = jnp.zeros((total_rows, rank), jnp.float32)
    for step in range(1, count):
        held, starts = arrived, starts_at(step)
        if step < count - 1:
            arrived = {key: hop(values, key[0]) for key, values in held.items()}
        blocks = [pair(held, i) for i in range(2)]
        low = put(low, first_products(blocks, starts), starts)
        products = [query_product(blocks[i], i) for i in range(2)]
        if step < count - 1:
            base = put(base, products[0] + products[1], starts)
        if step == min(OWN_STEP, count - 2):
            mine = [tied(mine[i], products[i]) for i in range(2)]
            low = put(low, first_products(mine, starts_at(0)), starts_at(0))
            base = put(base, query_product(mine[0], 0) + query_product(mine[1], 1), starts_at(0))
        if step < count - 1:
            for i in range(2):
                (arrived[1, i], arrived[-1, i]), products[i] = lax.optimization_barrier(
                    ((arrived[1, i], arrived[-1, i]), products[i])
                )

    low = jnp.concatenate([low[: total_rows // 2], low[total_rows // 2 :]], axis=1).astype(jnp.bfloat16)
    if count & (count - 1) == 0:
        distance = 1
        while distance < count:
            other = lax.ppermute(low, "tensor", [(i, i ^ distance) for i in range(count)])
            low = (low.astype(jnp.float32) + other.astype(jnp.float32)).astype(jnp.bfloat16)
            distance *= 2
    else:
        low = lax.psum(low, "tensor")
    low = jnp.concatenate([low[:, :rank], low[:, rank:]], axis=0)
    base = put(base, products[0] + products[1], starts)
    spread = (jnp.concatenate([low] * requests, axis=1).astype(jnp.float32) * member).astype(jnp.bfloat16)
    adapter_update = jnp.dot(
        spread, up_factor.reshape(requests * rank, width), preferred_element_type=jnp.float32
    )
    query = ((base + adapter_scale * adapter_update) * live[:, :1]).astype(jnp.bfloat16)
    return (hidden[None], query[None])


def solution(mesh):
    in_specs = (
        P("replica", "groups", "tensor"),
        P("replica", ("groups", "tensor"), None),
        P("tensor", None),
        P(None, "tensor"),
        P(),
        P("replica", "tensor", None),
        P("replica", None, "tensor"),
        P("replica", "groups"),
        P("replica", "groups"),
        P("replica", "groups"),
    )
    out_specs = (P("replica", ("groups", "tensor"), None), P("replica", "groups", "tensor"))
    return jax.shard_map(
        on_device, mesh=mesh, in_specs=in_specs, out_specs=out_specs, check_vma=False
    )
```

```python
import jax
import jax.numpy as jnp
from jax import lax
from jax.experimental import pallas as pl
from jax.experimental.pallas import tpu as pltpu
from jax.sharding import PartitionSpec as P

TILE = 64
STREAMS = 2
OWN_STEP = 4
adapter_scale = 2.0


def tied(values, after):
    return lax.optimization_barrier((values, after))[0]


def ring_order(count):
    if count % 2 or count > 8:
        return list(range(count))
    return list(range(0, count, 2)) + list(range(count - 1, 0, -2))


def swapped(values, replicas, shift):
    return lax.ppermute(values, "replica", [(i, (i + shift) % replicas) for i in range(replicas)])


def row_maps_kernel(requests, rank, tiles_ref, padding_ref, member_ref, live_ref):
    at = lax.broadcasted_iota(jnp.int32, member_ref.shape, 0)
    column = lax.broadcasted_iota(jnp.int32, member_ref.shape, 1)
    member = jnp.zeros(member_ref.shape, jnp.float32)
    row = lax.broadcasted_iota(jnp.int32, live_ref.shape, 0)
    live = jnp.zeros(live_ref.shape, jnp.float32)
    start = jnp.int32(0)
    for j in range(requests):
        end = start + tiles_ref[j] * TILE
        mine = (column >= j * rank) & (column < (j + 1) * rank)
        member = jnp.where(mine & (at >= start) & (at < end), 1.0, member)
        live = jnp.where((row >= start) & (row < end - padding_ref[j]), 1.0, live)
        start = end
    member_ref[...] = member
    live_ref[...] = live


def row_maps(tile_count, padding, total_rows, rank):
    requests = tile_count.shape[0]
    return pl.pallas_call(
        lambda *refs: row_maps_kernel(requests, rank, *refs),
        in_specs=[pl.BlockSpec(memory_space=pltpu.SMEM)] * 2,
        out_specs=[pl.BlockSpec(memory_space=pltpu.VMEM)] * 2,
        out_shape=[
            jax.ShapeDtypeStruct((total_rows, requests * rank), jnp.float32),
            jax.ShapeDtypeStruct((total_rows, 128), jnp.float32),
        ],
    )(tile_count, padding)


def fetched(store, picked, asked):
    resident = store.shape[0]
    replicas = lax.axis_size("replica")
    mine = lax.axis_index("replica")
    holder = picked // resident

    def held(wanted):
        here = wanted // resident == mine
        return store[jnp.where(here, wanted - mine * resident, 0)]

    factor = held(picked)
    for shift in range(1, replicas):
        from_peer = (holder == (mine - shift) % replicas)[:, None, None]
        factor = jnp.where(from_peer, swapped(held(asked[shift]), replicas, shift), factor)
    return factor


def on_device(
    attention_output_rows,
    residual,
    output_projection_weight,
    next_query_weight,
    input_norm_gain,
    adapter_down_weight,
    adapter_up_weight,
    request_adapter_index,
    request_tile_count,
    request_tail_padding,
):
    features = attention_output_rows[0]
    total_rows = features.shape[0]
    depth, model = output_projection_weight.shape
    width = next_query_weight.shape[1]
    rank = adapter_down_weight.shape[2]
    count = lax.axis_size("tensor")
    index = lax.axis_index("tensor")
    rows = total_rows // count
    order = ring_order(count)

    def wrapped(at):
        return at & (count - 1) if count & (count - 1) == 0 else lax.rem(at, count)

    if order[-1] == 1:
        place = jnp.where(index & 1 == 1, count - 1 - index // 2, index // 2)
    else:
        place = index

    def block_at(at):
        at = wrapped(at + 2 * count)
        if order[-1] == 1:
            at = jnp.where(at < count // 2, 2 * at, 2 * (count - 1 - at) + 1)
        return at

    def first_row(at):
        return block_at(at) * rows

    def hop(values, way):
        pairs = [(order[i], order[(i + way) % count]) for i in range(count)]
        return lax.ppermute(values, "tensor", pairs)

    ways = (1, -1)
    half = model // 2
    piece = half // STREAMS

    def block_of(product, way, step):
        return lax.dynamic_slice_in_dim(product, first_row(place - way * (1 + step)), rows, 0)

    picked_adapter = request_adapter_index[0]
    requests = picked_adapter.shape[0]

    replicas = lax.axis_size("replica")
    asked = {shift: swapped(picked_adapter, replicas, -shift) for shift in range(1, replicas)}
    down_factor = up_factor = None

    own, held, before = {}, {}, None
    for i in range(STREAMS):
        for way in ways:
            source = features if before is None else tied(features, before)
            lower = (0 if way == 1 else half) + i * piece
            weight = output_projection_weight[:, lower : lower + piece]
            before = jnp.dot(source, weight, preferred_element_type=jnp.float32).astype(jnp.bfloat16)
            own[way, i], held[way, i] = before, block_of(before, way, 0)
    for step in range(count - 1):
        if step == 2:
            down_factor = fetched(tied(adapter_down_weight, held[-1,0]), picked_adapter, asked)
        if step == 3:
            up_factor = fetched(tied(adapter_up_weight, held[-1,0]), picked_adapter, asked)
        if step == 4:
            maps = tied((request_tile_count[0], request_tail_padding[0]), held[-1,0])
            member, live = row_maps(*maps, total_rows, rank)
        if step == 4:
            held[-1,0], down_factor = lax.optimization_barrier((held[-1,0], down_factor))
        if step == 5:
            held[-1,0], up_factor = lax.optimization_barrier((held[-1,0], up_factor))
        if step == 6:
            held[-1,0], member, live = lax.optimization_barrier((held[-1,0], member, live))
        for i in range(STREAMS):
            for way in ways:
                term = block_of(own[way, i], way, step + 1).astype(jnp.float32)
                arrived = hop(held[way, i], way).astype(jnp.float32) + term
                held[way, i] = arrived if step == count - 2 else arrived.astype(jnp.bfloat16)
    hidden = (residual[0].astype(jnp.float32) + jnp.concatenate([held[way, i] for way in ways for i in range(STREAMS)], axis=1)).astype(jnp.bfloat16)
    values = hidden.astype(jnp.float32)
    scale = lax.rsqrt(jnp.mean(values * values, axis=-1, keepdims=True) + 1e-05)
    normed = (values * scale * input_norm_gain[None, :]).astype(jnp.bfloat16)

    def lower_of(way):
        return 0 if way == 1 else half

    held = {}
    for i in range(STREAMS):
        for way in ways:
            lower = lower_of(way) + i * piece
            held[way, i] = normed[:, lower : lower + piece]
    arrived = {key: hop(values, key[0]) for key, values in held.items()}
    (arrived[1, 0], arrived[-1, 0]), hidden = lax.optimization_barrier(((arrived[1, 0], arrived[-1, 0]), hidden))
    flat_down = jnp.transpose(down_factor, (1, 0, 2)).reshape(depth, requests * rank)
    base = jnp.zeros((total_rows, width), jnp.float32)

    def added(whole, values, start):
        before = lax.dynamic_slice_in_dim(whole, start, rows, 0)
        return lax.dynamic_update_slice_in_dim(whole, before + values, start, 0)

    def first_products(blocks, step):
        forward = index * depth < half
        lower = jnp.where(forward, index * depth, index * depth - half)
        parts = [lax.dynamic_slice_in_dim(blocks[way], lower, depth, 1) for way in ways]
        part = jnp.where(forward, parts[0], parts[1])
        start = first_row(jnp.where(forward, place - step, place + step))
        product = jnp.dot(part, flat_down, preferred_element_type=jnp.float32)
        product = product * lax.dynamic_slice_in_dim(member, start, rows, 0)
        return sum(product[:, j * rank : (j + 1) * rank] for j in range(requests)), start

    def query_product(block, way):
        weight = next_query_weight[lower_of(way) : lower_of(way) + half]
        return jnp.dot(block, weight, preferred_element_type=jnp.float32)

    def whole_of(values, way):
        return jnp.concatenate([values[way, i] for i in range(STREAMS)], axis=1)

    mine = {way: whole_of(held, way) for way in ways}
    low = jnp.zeros((total_rows, rank), jnp.float32)
    for step in range(1, count):
        held = arrived
        if step < count - 1:
            arrived = {key: hop(values, key[0]) for key, values in held.items()}
        blocks = {way: whole_of(held, way) for way in ways}
        picked, start = first_products(blocks, step)
        low = lax.dynamic_update_slice_in_dim(low, picked, start, 0)
        products = {way: query_product(blocks[way], way) for way in ways}
        if step < count - 1:
            for way in ways:
                base = added(base, products[way], first_row(place - way * step))
        if step == min(OWN_STEP, count - 2):
            mine = {way: tied(mine[way], products[way]) for way in ways}
            picked, start = first_products(mine, 0)
            low = lax.dynamic_update_slice_in_dim(low, picked, start, 0)
            base = added(base, query_product(mine[1], 1) + query_product(mine[-1], -1), first_row(place))
        if step < count - 1:
            for i, way in enumerate(ways):
                (arrived[1, i], arrived[-1, i]), products[way] = lax.optimization_barrier(
                    ((arrived[1, i], arrived[-1, i]), products[way])
                )

    low = jnp.concatenate([low[: total_rows // 2], low[total_rows // 2 :]], axis=1).astype(jnp.bfloat16)
    if count & (count - 1) == 0:
        distance = 1
        while distance < count:
            other = lax.ppermute(low, "tensor", [(i, i ^ distance) for i in range(count)])
            low = (low.astype(jnp.float32) + other.astype(jnp.float32)).astype(jnp.bfloat16)
            distance *= 2
    else:
        low = lax.psum(low, "tensor")
    low = jnp.concatenate([low[:, :rank], low[:, rank:]], axis=0)
    for way in ways:
        base = added(base, products[way], first_row(place - way * (count - 1)))
    spread = (jnp.concatenate([low] * requests, axis=1).astype(jnp.float32) * member).astype(jnp.bfloat16)
    adapter_update = jnp.dot(
        spread, up_factor.reshape(requests * rank, width), preferred_element_type=jnp.float32
    )
    query = ((base + adapter_scale * adapter_update) * live[:, :1]).astype(jnp.bfloat16)
    return (hidden[None], query[None])


def solution(mesh):
    in_specs = (
        P("replica", "groups", "tensor"),
        P("replica", ("groups", "tensor"), None),
        P("tensor", None),
        P(None, "tensor"),
        P(),
        P("replica", "tensor", None),
        P("replica", None, "tensor"),
        P("replica", "groups"),
        P("replica", "groups"),
        P("replica", "groups"),
    )
    out_specs = (P("replica", ("groups", "tensor"), None), P("replica", "groups", "tensor"))
    return jax.shard_map(
        on_device, mesh=mesh, in_specs=in_specs, out_specs=out_specs, check_vma=False
    )
```
